512 devices in a mesh: tile: 8 (over y, core), depth: 64 (over x, z).
Axes of the slice: x: 4, y: 4, z: 16, core: 2. Of those that a mesh axis runs over, the one named last changes fastest.
Arguments:
- volume: int32 [512, 128, 2048], P('depth', None, 'tile'), may hold values from 0 to 255
- colors: float32 [3, 256], replicated, may hold values from 0 to 1
- extinction: float32 [256], replicated, may hold values from 0.25 to 256
Outputs:
- frame: float32 [4, 128, 2048], P(None, 'depth')
The draws below stay inside these ranges and needn't reach their ends.
All inputs are finite; a program needn't handle non-finite values.
Results may differ from the reference program's by a relative error of at most 0.0016.
Values sent between devices are 32-bit elements; how exact they have to be, the bound alone decides.
No kernel may reach another device: no remote copies, remote signals or barrier semaphores. Data moves between devices by JAX's collectives and lax.ppermute only.
A program may use at most 64 MiB of HBM per device.

```python
import math
import jax
import jax.numpy as jnp
from jax import lax

ROWS = 128
BINS = 256
NZ = 512
WIDTH = 2048


def draw_volume(key, part):
    key = jax.random.fold_in(key, 11)
    base_key, offset_key, pick_key, free_key = jax.random.split(key, 4)
    spread = max(BINS // 8, 2)
    ray_base = jax.random.randint(base_key, (ROWS, WIDTH), 0, BINS)
    offsets = jax.random.randint(offset_key, (NZ, ROWS, WIDTH), 0, spread)
    scattered = jax.random.randint(pick_key, (NZ, ROWS, WIDTH), 0, 8) == 0
    free_bins = jax.random.randint(free_key, (NZ, ROWS, WIDTH), 0, BINS)
    local_bins = (ray_base[None, :, :] + offsets) % BINS
    return jnp.where(scattered, free_bins, local_bins).astype(jnp.int32)


def draw_extinction(key, part):
    key = jax.random.fold_in(key, 23)
    base_key, pick_key, dense_key = jax.random.split(key, 3)
    dense_count = max(BINS // 32, 1)
    order = jax.random.permutation(pick_key, BINS)
    dense = order < dense_count
    common = jnp.exp(jax.random.uniform(base_key, (BINS,), jnp.float32, math.log(0.25), math.log(4.0)))
    heavy = jax.random.uniform(dense_key, (BINS,), jnp.float32, 0.1, 0.4) * NZ
    return jnp.where(dense, heavy, common).astype(jnp.float32)


def setup_inputs(seed: int = 0) -> dict:
    splits = jax.random.split(jax.random.key(seed), 4)
    return {
        "volume": draw_volume(jax.random.fold_in(splits[3], 71), 0),
        "colors": jnp.clip(jax.random.uniform(splits[1], (3, BINS), jnp.float32, 0.0, 1.0), 0.0, 1.0),
        "extinction": draw_extinction(jax.random.fold_in(splits[3], 71), 0),
    }


def make_table(colors, extinction, depth_total):
    opacity = 1.0 - jnp.exp(-extinction / depth_total)
    return jnp.concatenate([colors * opacity[None, :], opacity[None, :]], axis=0).astype(jnp.bfloat16)


def blend_over(front_part, back_part, channel_axis):
    opacity = lax.slice_in_dim(front_part, 3, 4, axis=channel_axis)
    return front_part + (1.0 - opacity) * back_part


def reference(volume, colors, extinction):
    color_table = lax.optimization_barrier(make_table(colors, extinction, NZ))

    def marching(accumulated, bin_slice):
        samples = jnp.take(color_table, bin_slice, axis=1).astype(jnp.float32)
        return blend_over(accumulated, samples, 0), None

    initial = jnp.zeros((4, ROWS, WIDTH), jnp.float32)
    image, _ = lax.scan(marching, initial, volume)
    return image
```

```python
import functools

import jax
import jax.numpy as jnp
from jax import lax
from jax.experimental import pallas as pl
from jax.experimental.pallas import tpu as pltpu
from jax.sharding import PartitionSpec as P

LANES = 128
VMEM = pl.BlockSpec(memory_space=pltpu.VMEM)


def lookup(halves, bins, high):
    low_part = jnp.take_along_axis(halves[0], bins, axis=1, mode="promise_in_bounds")
    high_part = jnp.take_along_axis(halves[1], bins, axis=1, mode="promise_in_bounds")
    return jnp.where(high, high_part, low_part)


def table_rows(colors_ref, extinction_ref, depth_total):
    opacity = 1.0 - jnp.exp(-extinction_ref[...] / depth_total)
    rows = [colors_ref[c : c + 1, :] * opacity for c in range(3)] + [opacity]
    rows = [row.astype(jnp.bfloat16).astype(jnp.float32) for row in rows]
    return [
        [jnp.broadcast_to(row[:, h * LANES : (h + 1) * LANES], (8, LANES)) for h in range(2)]
        for row in rows
    ]


def march_kernel(colors_ref, extinction_ref, volume_ref, out_ref, *, depth_total):
    depth_cells, row_count, col_count = volume_ref.shape
    table = table_rows(colors_ref, extinction_ref, depth_total)
    col_blocks = col_count // LANES

    def step(i, carry):
        block = i // col_blocks
        row = pl.multiple_of(block * 8, 8)
        col = pl.multiple_of(i % col_blocks * LANES, LANES)
        image, clear = None, None
        for z in range(depth_cells):
            bins = volume_ref[z, pl.ds(row, 8), pl.ds(col, LANES)]
            high = bins >= LANES
            low_bits = bins & (LANES - 1)
            sample = [lookup(halves, low_bits, high) for halves in table]
            if z == 0:
                image = sample
            else:
                image = [a + clear * s for a, s in zip(image, sample)]
            clear = 1.0 - image[3]
        for c in range(4):
            for k in range(4):
                out_ref[block * 4 + k, 2 * c : 2 * c + 2, pl.ds(col, LANES)] = image[c][2 * k : 2 * k + 2]
        return carry

    lax.fori_loop(0, row_count // 8 * col_blocks, step, 0, unroll=4)


def blend_packed(front, back):
    sub = lax.broadcasted_iota(jnp.int32, front.shape, 0)
    opacity = jnp.where(sub >= 6, front, 0.0)
    opacity = opacity + pltpu.roll(opacity, 4, 0)
    opacity = opacity + pltpu.roll(opacity, 2, 0)
    return front + (1.0 - opacity) * back


def fold(parts_ref, lo, hi, col):
    if hi - lo == 1:
        return parts_ref[lo, :, pl.ds(col, LANES)]
    mid = (lo + hi) // 2
    return blend_packed(fold(parts_ref, lo, mid, col), fold(parts_ref, mid, hi, col))


def fold_kernel(parts_ref, out_ref):
    count, _, col_count = parts_ref.shape
    for col in range(0, col_count, LANES):
        image = fold(parts_ref, 0, count, col)
        for t in range(out_ref.shape[0]):
            out_ref[t, :, pl.ds(col, LANES)] = image


def assemble_kernel(strips_ref, out_ref):
    count, _, col_count = strips_ref.shape
    for t in range(count):
        for c in range(4):
            out_ref[c, :, pl.ds(t * col_count, col_count)] = strips_ref[t, 2 * c : 2 * c + 2, :]


def body(volume, colors, extinction):
    depth_count = lax.axis_size("depth")
    tile_count = lax.axis_size("tile")
    depth_cells, row_count, col_count = volume.shape
    f32 = jnp.float32
    partial_image = pl.pallas_call(
        functools.partial(march_kernel, depth_total=depth_cells * depth_count),
        out_shape=jax.ShapeDtypeStruct((row_count // 2, 8, col_count), f32),
        in_specs=[VMEM, VMEM, VMEM],
        out_specs=VMEM,
        name="march",
    )(colors, extinction.reshape(1, -1), volume)
    parts = lax.all_to_all(partial_image, "depth", split_axis=0, concat_axis=0, tiled=True)
    strip = pl.pallas_call(
        fold_kernel,
        out_shape=jax.ShapeDtypeStruct((tile_count, 8, col_count), f32),
        in_specs=[VMEM],
        out_specs=VMEM,
        name="fold",
    )(parts)
    strips = lax.all_to_all(strip, "tile", split_axis=0, concat_axis=0, tiled=True)
    return pl.pallas_call(
        assemble_kernel,
        out_shape=jax.ShapeDtypeStruct((4, 2, tile_count * col_count), f32),
        in_specs=[VMEM],
        out_specs=VMEM,
        name="assemble",
    )(strips)


def solution(mesh):
    in_specs = (P("depth", None, "tile"), P(), P())
    out_specs = P(None, "depth", None)
    return jax.shard_map(body, mesh=mesh, in_specs=in_specs, out_specs=out_specs, check_vma=False)
```

```python
import functools

import jax
import jax.numpy as jnp
from jax import lax
from jax.experimental import pallas as pl
from jax.experimental.pallas import tpu as pltpu
from jax.sharding import PartitionSpec as P

LANES = 128
VMEM = pl.BlockSpec(memory_space=pltpu.VMEM)
PARAMS = pltpu.CompilerParams(vmem_limit_bytes=16 * 2**20)


def lookup(halves, bins, high):
    low_part = jnp.take_along_axis(halves[0], bins, axis=1, mode="promise_in_bounds")
    high_part = jnp.take_along_axis(halves[1], bins, axis=1, mode="promise_in_bounds")
    return jnp.where(high, high_part, low_part)


def table_rows(colors_ref, extinction_ref, depth_total):
    opacity = 1.0 - jnp.exp(-extinction_ref[...] / depth_total)
    rows = [colors_ref[c : c + 1, :] * opacity for c in range(3)] + [opacity]
    rows = [row.astype(jnp.bfloat16).astype(jnp.float32) for row in rows]
    return [
        [jnp.broadcast_to(row[:, h * LANES : (h + 1) * LANES], (8, LANES)) for h in range(2)]
        for row in rows
    ]


def march_kernel(colors_ref, extinction_ref, volume_ref, out_ref, *, depth_total, partner):
    depth_cells, row_count, col_count = volume_ref.shape
    table = table_rows(colors_ref, extinction_ref, depth_total)
    col_blocks = col_count // LANES
    parity = (lax.axis_index("depth") + partner) % 2
    sub = lax.broadcasted_iota(jnp.int32, (8, LANES), 0)
    first = (sub // 2) % 2 == parity

    def step(i, carry):
        block = i // col_blocks
        row = pl.multiple_of(block * 16, 16)
        col = pl.multiple_of(i % col_blocks * LANES, LANES)
        image, clear = None, None
        for z in range(depth_cells):
            a = volume_ref[z, pl.ds(row, 8), pl.ds(col, LANES)]
            b = volume_ref[z, pl.ds(row + 8, 8), pl.ds(col, LANES)]
            bins = jnp.where(first, a, pltpu.roll(b, 2, 0))
            high = bins >= LANES
            low_bits = bins & (LANES - 1)
            sample = [lookup(halves, low_bits, high) for halves in table]
            if z == 0:
                image = sample
            else:
                image = [x + clear * s for x, s in zip(image, sample)]
            clear = 1.0 - image[3]
        for c in range(4):
            out_ref[c, pl.ds(pl.multiple_of(block * 8, 8), 8), pl.ds(col, LANES)] = image[c]
        return carry

    lax.fori_loop(0, row_count // 16 * col_blocks, step, 0, unroll=4)


def march(colors, extinction, volume, depth_total, partner):
    _, row_count, col_count = volume.shape
    return pl.pallas_call(
        functools.partial(march_kernel, depth_total=depth_total, partner=partner),
        out_shape=jax.ShapeDtypeStruct((4, row_count // 2, col_count), jnp.float32),
        in_specs=[VMEM, VMEM, VMEM],
        out_specs=VMEM,
        compiler_params=PARAMS,
        cost_estimate=pl.CostEstimate(flops=20_000_000, bytes_accessed=8_000_000, transcendentals=0),
        name="march_partner" if partner else "march_own",
    )(colors, extinction, volume)


def merge_kernel(own_ref, other_ref, out_ref):
    _, row_count, col_count = own_ref.shape
    parity = lax.axis_index("depth") % 2
    even = jnp.full((8, LANES), parity) == 0
    places = [jnp.where(parity == 0, e, o) for e, o in zip((0, 2, 1, 3), (3, 0, 2, 1))]
    for block in range(row_count // 8):
        for col in range(0, col_count, LANES):
            at = (pl.ds(block * 8, 8), pl.ds(col, LANES))
            own = [own_ref[c, *at] for c in range(4)]
            other = [other_ref[c, *at] for c in range(4)]
            front = [jnp.where(even, x, y) for x, y in zip(own, other)]
            back = [jnp.where(even, y, x) for x, y in zip(own, other)]
            clear = 1.0 - front[3]
            for c in range(4):
                image = front[c] + clear * back[c]
                for k in range(4):
                    out_ref[4 * block + places[k], 2 * c : 2 * c + 2, pl.ds(col, LANES)] = image[2 * k : 2 * k + 2]


def blend_packed(front, back):
    sub = lax.broadcasted_iota(jnp.int32, front.shape, 0)
    opacity = jnp.where(sub >= 6, front, 0.0)
    opacity = opacity + pltpu.roll(opacity, 4, 0)
    opacity = opacity + pltpu.roll(opacity, 2, 0)
    return front + (1.0 - opacity) * back


def fold(parts_ref, lo, hi, col):
    if hi - lo == 1:
        return parts_ref[lo, :, pl.ds(col, LANES)]
    mid = (lo + hi) // 2
    return blend_packed(fold(parts_ref, lo, mid, col), fold(parts_ref, mid, hi, col))


def fold_kernel(parts_ref, out_ref):
    count, _, col_count = parts_ref.shape
    for col in range(0, col_count, LANES):
        image = fold(parts_ref, 0, count, col)
        for t in range(out_ref.shape[0]):
            out_ref[t, :, pl.ds(col, LANES)] = image


def assemble_kernel(strips_ref, out_ref):
    count, _, col_count = strips_ref.shape
    for t in range(count):
        for c in range(4):
            out_ref[c, :, pl.ds(t * col_count, col_count)] = strips_ref[t, 2 * c : 2 * c + 2, :]


def body(volume, colors, extinction):
    depth_count = lax.axis_size("depth")
    tile_count = lax.axis_size("tile")
    depth_cells, row_count, col_count = volume.shape
    f32 = jnp.float32
    depth_total = depth_cells * depth_count
    extinction = extinction.reshape(1, -1)
    outgoing = march(colors, extinction, volume, depth_total, 1)
    other = lax.ppermute(outgoing, "depth", [(d, d ^ 1) for d in range(depth_count)])
    own = march(colors, extinction, volume, depth_total, 0)
    pair = pl.pallas_call(
        merge_kernel,
        out_shape=jax.ShapeDtypeStruct((row_count // 4, 8, col_count), f32),
        in_specs=[VMEM, VMEM],
        out_specs=VMEM,
        compiler_params=PARAMS,
        name="merge",
    )(own, other)
    groups = [list(range(p, depth_count, 2)) for p in range(2)]
    parts = lax.all_to_all(
        pair, "depth", split_axis=0, concat_axis=0, tiled=True, axis_index_groups=groups
    )
    strip = pl.pallas_call(
        fold_kernel,
        out_shape=jax.ShapeDtypeStruct((tile_count, 8, col_count), f32),
        in_specs=[VMEM],
        out_specs=VMEM,
        compiler_params=PARAMS,
        name="fold",
    )(parts)
    strips = lax.all_to_all(strip, "tile", split_axis=0, concat_axis=0, tiled=True)
    return pl.pallas_call(
        assemble_kernel,
        out_shape=jax.ShapeDtypeStruct((4, 2, tile_count * col_count), f32),
        in_specs=[VMEM],
        out_specs=VMEM,
        compiler_params=PARAMS,
        name="assemble",
    )(strips)


def solution(mesh):
    in_specs = (P("depth", None, "tile"), P(), P())
    out_specs = P(None, "depth", None)
    return jax.shard_map(body, mesh=mesh, in_specs=in_specs, out_specs=out_specs, check_vma=False)
```

```python
import functools

import jax
import jax.numpy as jnp
from jax import lax
from jax.experimental import pallas as pl
from jax.experimental.pallas import tpu as pltpu
from jax.sharding import Mesh
from jax.sharding import PartitionSpec as P

LANES = 128
SIDES = 2
DEPTH = ("pair", "side")
PIECES = 4
RING = 16
VMEM = pl.BlockSpec(memory_space=pltpu.VMEM)
ANY = pl.BlockSpec(memory_space=pl.ANY)
SMALL = 16 * 2**20
LARGE = 127 * 2**19


def send_order(depth_count, ring):
    half = ring // 2
    slabs = depth_count // ring
    return [x * half + (z + half // 2) % half for z in range(half) for x in reversed(range(slabs))]


def lookup(halves, bins, high):
    low_part = jnp.take_along_axis(halves[0], bins, axis=1, mode="promise_in_bounds")
    high_part = jnp.take_along_axis(halves[1], bins, axis=1, mode="promise_in_bounds")
    return jnp.where(high, high_part, low_part)


def table_rows(colors, extinction, depth_total):
    opacity = 1.0 - jnp.exp(-extinction / depth_total)
    rows = [colors[c : c + 1, :] * opacity for c in range(3)] + [opacity]
    rows = [row.astype(jnp.bfloat16).astype(jnp.float32) for row in rows]
    return [
        [jnp.broadcast_to(row[:, h * LANES : (h + 1) * LANES], (8, LANES)) for h in range(2)]
        for row in rows
    ]


def march_rows(table, volume_ref, out_ref, side, lo, hi):
    depth_cells, _, col_count = volume_ref.shape
    col_blocks = col_count // LANES
    place = lax.broadcasted_iota(jnp.int32, (8, LANES), 0) // 2 % SIDES
    takes = [place == (side + j) % SIDES for j in range(1, SIDES)]

    def step(i, carry):
        block = i // col_blocks
        row = pl.multiple_of(block * 8 * SIDES, 8 * SIDES)
        col = pl.multiple_of(i % col_blocks * LANES, LANES)
        image, clear = None, None
        for z in range(depth_cells):
            bins = volume_ref[z, pl.ds(row, 8), pl.ds(col, LANES)]
            for j in range(1, SIDES):
                other = volume_ref[z, pl.ds(row + 8 * j, 8), pl.ds(col, LANES)]
                bins = jnp.where(takes[j - 1], pltpu.roll(other, 2 * j, 0), bins)
            high = bins >= LANES
            low_bits = bins & (LANES - 1)
            sample = [lookup(halves, low_bits, high) for halves in table]
            if z == 0:
                image = sample
            else:
                image = [x + clear * s for x, s in zip(image, sample)]
            clear = 1.0 - image[3]
        for c in range(4):
            out_ref[c, pl.ds(pl.multiple_of(block * 8, 8), 8), pl.ds(col, LANES)] = image[c]
        return carry

    lax.fori_loop(lo * col_blocks, hi * col_blocks, step, 0, unroll=4)


def early_kernel(
    colors_any,
    extinction_any,
    volume_any,
    out_any,
    colors_ref,
    extinction_ref,
    volume_ref,
    out_ref,
    sems,
    *,
    depth_total,
    swap,
):
    piece = volume_ref.shape[1] // PIECES
    copies = [
        pltpu.make_async_copy(colors_any, colors_ref, sems.at[0]),
        pltpu.make_async_copy(extinction_any, extinction_ref, sems.at[1]),
    ]
    for k in range(PIECES):
        rows = pl.ds(k * piece, piece)
        copies.append(
            pltpu.make_async_copy(volume_any.at[:, rows, :], volume_ref.at[:, rows, :], sems.at[2 + k])
        )
    for copy in copies:
        copy.start()
    copies[0].wait()
    copies[1].wait()
    table = table_rows(colors_ref[...], extinction_ref[...], depth_total)
    for k in range(PIECES):
        copies[2 + k].wait()
        march_rows(table, volume_ref, out_ref, lax.axis_index("side") ^ swap, k * piece // 16, (k + 1) * piece // 16)
        rows = pl.ds(k * piece // 2, piece // 2)
        copies.append(
            pltpu.make_async_copy(out_ref.at[:, rows, :], out_any.at[:, rows, :], sems.at[2 + PIECES + k])
        )
        copies[-1].start()
    for copy in copies[2 + PIECES :]:
        copy.wait()


def late_kernel(colors_ref, extinction_ref, volume_ref, out_ref, *, depth_total, swap):
    table = table_rows(colors_ref[...], extinction_ref[...], depth_total)
    march_rows(table, volume_ref, out_ref, lax.axis_index("side") ^ swap, 0, volume_ref.shape[1] // 16)


def march(colors, extinction, volume, depth_total, swap):
    depth_cells, row_count, col_count = volume.shape
    early = swap != 0
    scratch = [
        pltpu.VMEM(colors.shape, jnp.float32),
        pltpu.VMEM(extinction.shape, jnp.float32),
        pltpu.VMEM(volume.shape, jnp.int32),
        pltpu.VMEM((4, row_count // 2, col_count), jnp.float32),
        pltpu.SemaphoreType.DMA((2 + 2 * PIECES,)),
    ]
    return pl.pallas_call(
        functools.partial(early_kernel if early else late_kernel, depth_total=depth_total, swap=swap),
        out_shape=jax.ShapeDtypeStruct((4, row_count // 2, col_count), jnp.float32),
        in_specs=[ANY if early else VMEM] * 3,
        out_specs=ANY if early else VMEM,
        scratch_shapes=scratch if early else (),
        compiler_params=pltpu.CompilerParams(vmem_limit_bytes=LARGE if early else SMALL),
        cost_estimate=pl.CostEstimate(flops=20_000_000, bytes_accessed=8_000_000, transcendentals=0),
        name="march_side%d" % swap,
    )(colors, extinction, volume)


def blend(front, back):
    clear = 1.0 - front[3]
    return [f + clear * b for f, b in zip(front, back)]


def merge_kernel(own_ref, other_ref, out_ref, *, slots):
    _, row_count, col_count = own_ref.shape
    side = lax.axis_index("side")
    odd = jnp.full((8, LANES), side) == 1
    for block in range(row_count // 8):
        places = [
            jnp.where(side == 0, slots[4 * block + even], slots[4 * block + uneven])
            for even, uneven in zip((0, 2, 1, 3), (3, 0, 2, 1))
        ]
        for col in range(0, col_count, LANES):
            at = (pl.ds(block * 8, 8), pl.ds(col, LANES))
            own = [own_ref[c, *at] for c in range(4)]
            other = [other_ref[c, *at] for c in range(4)]
            image = blend(
                [jnp.where(odd, y, x) for x, y in zip(own, other)],
                [jnp.where(odd, x, y) for x, y in zip(own, other)],
            )
            for k in range(4):
                for c in range(4):
                    out_ref[places[k], 2 * c : 2 * c + 2, pl.ds(col, LANES)] = image[c][2 * k : 2 * k + 2]


def blend_packed(front, back):
    sub = lax.broadcasted_iota(jnp.int32, front.shape, 0)
    opacity = jnp.where(sub >= 6, front, 0.0)
    opacity = opacity + pltpu.roll(opacity, 4, 0)
    opacity = opacity + pltpu.roll(opacity, 2, 0)
    return front + (1.0 - opacity) * back


def fold(parts):
    while len(parts) > 1:
        parts = [blend_packed(f, b) for f, b in zip(parts[0::2], parts[1::2])]
    return parts[0]


def fold_kernel(parts_ref, out_ref, *, slots):
    _, _, col_count = parts_ref.shape
    for col in range(0, col_count, LANES):
        image = fold([parts_ref[slot, :, pl.ds(col, LANES)] for slot in slots])
        for t in range(out_ref.shape[0]):
            out_ref[t, :, pl.ds(col, LANES)] = image


def assemble_kernel(strips_ref, out_ref):
    count, _, col_count = strips_ref.shape
    for t in range(count):
        for c in range(4):
            out_ref[c, :, pl.ds(t * col_count, col_count)] = strips_ref[count - 1 - t, 2 * c : 2 * c + 2, :]


def small_call(kernel, out_shape, name, *args):
    return pl.pallas_call(
        kernel,
        out_shape=jax.ShapeDtypeStruct(out_shape, jnp.float32),
        in_specs=[VMEM] * len(args),
        out_specs=VMEM,
        compiler_params=pltpu.CompilerParams(vmem_limit_bytes=SMALL),
        name=name,
    )(*args)


def body(volume, colors, extinction):
    tile_count = lax.axis_size("tile")
    pair_count = lax.axis_size("pair")
    depth_cells, row_count, col_count = volume.shape
    depth_total = depth_cells * 2 * pair_count
    extinction = extinction.reshape(1, -1)
    order = send_order(2 * pair_count, RING)
    slots = [order.index(pair) for pair in range(pair_count)]

    outgoing = march(colors, extinction, volume, depth_total, 1)
    other = lax.ppermute(outgoing, "side", [(0, 1), (1, 0)])
    own = march(colors, extinction, volume, depth_total, 0)
    merge = functools.partial(merge_kernel, slots=slots)
    image = small_call(merge, (row_count // 4, 8, col_count), "merge", own, other)
    parts = lax.all_to_all(image, "pair", split_axis=0, concat_axis=0, tiled=True, axis_index_groups=[order])
    fold_parts = functools.partial(fold_kernel, slots=slots)
    strip = small_call(fold_parts, (tile_count, 8, col_count), "fold", parts)
    tiles = list(reversed(range(tile_count)))
    strips = lax.all_to_all(strip, "tile", split_axis=0, concat_axis=0, tiled=True, axis_index_groups=[tiles])
    return small_call(assemble_kernel, (4, 2, tile_count * col_count), "assemble", strips)


def solution(mesh):
    tiles, depth = mesh.devices.shape
    mesh = Mesh(mesh.devices.reshape(tiles, depth // SIDES, SIDES), ("tile",) + DEPTH)
    in_specs = (P(DEPTH, None, "tile"), P(), P())
    out_specs = P(None, DEPTH, None)
    return jax.shard_map(body, mesh=mesh, in_specs=in_specs, out_specs=out_specs, check_vma=False)
```

```python
import functools

import jax
import jax.numpy as jnp
from jax import lax
from jax.experimental import pallas as pl
from jax.experimental.pallas import tpu as pltpu
from jax.sharding import Mesh
from jax.sharding import PartitionSpec as P

LANES = 128
SIDES = 2
DEPTH = ("pair", "side")
SLABS = 4
UNIT = 2.0**31
RANK = (5, 7, 4, 6, 1, 3, 0, 2)
VMEM = pl.BlockSpec(memory_space=pltpu.VMEM)
ANY = pl.BlockSpec(memory_space=pl.ANY)
SMALL = 16 * 2**20
LARGE = 2**26


def send_order():
    return [x * len(RANK) + z for z in RANK for x in reversed(range(SLABS))]


def lookup(halves, bins, high):
    low_part = jnp.take_along_axis(halves[0], bins, axis=1, mode="promise_in_bounds")
    high_part = jnp.take_along_axis(halves[1], bins, axis=1, mode="promise_in_bounds")
    return jnp.where(high, high_part, low_part)


def encode(row):
    whole = jnp.round(row * UNIT).astype(jnp.int32)
    shift = sum((whole >= 256 << k).astype(jnp.int32) for k in range(22))
    return (whole >> shift) | (shift << 8)


def decode(words):
    low = (words & 255) << ((words >> 8) & 31)
    high = ((words >> 13) & 255) << (words >> 21)
    return low.astype(jnp.float32), high.astype(jnp.float32)


def table_rows(colors, extinction, depth_total):
    opacity = 1.0 - jnp.exp(-extinction / depth_total)
    rows = [colors[c : c + 1, :] * opacity for c in range(3)] + [opacity]
    codes = [encode(row.astype(jnp.bfloat16).astype(jnp.float32)) for row in rows]
    words = [codes[0] | (codes[1] << 13), codes[2] | (codes[3] << 13)]
    return [
        [jnp.broadcast_to(word[:, h * LANES : (h + 1) * LANES], (8, LANES)) for h in range(2)]
        for word in words
    ]


def march_rows(table, volume_ref, out_ref, side, lo, hi):
    depth_cells, _, col_count = volume_ref.shape
    col_blocks = col_count // LANES
    place = lax.broadcasted_iota(jnp.int32, (8, LANES), 0) // 2 % SIDES
    takes = [place == (side + j) % SIDES for j in range(1, SIDES)]

    def step(i, carry):
        block = i // col_blocks
        row = pl.multiple_of(block * 8 * SIDES, 8 * SIDES)
        col = pl.multiple_of(i % col_blocks * LANES, LANES)
        image, clear = None, None
        for z in range(depth_cells):
            bins = volume_ref[z, pl.ds(row, 8), pl.ds(col, LANES)]
            for j in range(1, SIDES):
                other = volume_ref[z, pl.ds(row + 8 * j, 8), pl.ds(col, LANES)]
                bins = jnp.where(takes[j - 1], pltpu.roll(other, 2 * j, 0), bins)
            high = bins >= LANES
            low_bits = bins & (LANES - 1)
            sample = [x for halves in table for x in decode(lookup(halves, low_bits, high))]
            if z == 0:
                image = sample
            else:
                image = [x + clear * s for x, s in zip(image, sample)]
            clear = 1.0 - image[3] * (1 / UNIT)
        for c in range(4):
            out_ref[c, pl.ds(pl.multiple_of(block * 8, 8), 8), pl.ds(col, LANES)] = image[c] * (1 / UNIT)
        return carry

    lax.fori_loop(lo * col_blocks, hi * col_blocks, step, 0, unroll=4)


def march_all(table, volume_ref, out_ref, slab):
    depth_cells, _, col_count = volume_ref.shape

    def step(i, carry):
        col = pl.multiple_of(i * LANES, LANES)
        for j in range(4):
            row = (slab * 4 + j) * 8
            image, clear = None, None
            for z in range(depth_cells):
                bins = volume_ref[z, pl.ds(row, 8), pl.ds(col, LANES)]
                high = bins >= LANES
                low_bits = bins & (LANES - 1)
                sample = [x for halves in table for x in decode(lookup(halves, low_bits, high))]
                if z == 0:
                    image = sample
                else:
                    image = [x + clear * s for x, s in zip(image, sample)]
                clear = 1.0 - image[3] * (1 / UNIT)
            for c in range(4):
                done = image[c] * (1 / UNIT)
                for k in range(4):
                    place = (RANK.index(2 * j + k // 2), SLABS - 1 - slab, k % 2)
                    out_ref[*place, 2 * c : 2 * c + 2, pl.ds(col, LANES)] = done[2 * k : 2 * k + 2]
        return carry

    lax.fori_loop(0, col_count // LANES, step, 0)


def march_kernel(
    colors_any,
    extinction_any,
    volume_any,
    out_any,
    colors_ref,
    extinction_ref,
    volume_ref,
    out_ref,
    sems,
    *,
    depth_total,
    swap,
):
    piece = volume_ref.shape[1] // SLABS
    copies = [
        pltpu.make_async_copy(colors_any, colors_ref, sems.at[0]),
        pltpu.make_async_copy(extinction_any, extinction_ref, sems.at[1]),
    ]
    for k in range(SLABS):
        rows = pl.ds(k * piece, piece)
        copies.append(
            pltpu.make_async_copy(volume_any.at[:, rows, :], volume_ref.at[:, rows, :], sems.at[2 + k])
        )
    for copy in copies:
        copy.start()
    copies[0].wait()
    copies[1].wait()
    table = table_rows(colors_ref[...], extinction_ref[...], depth_total)
    for k in range(SLABS):
        copies[2 + k].wait()
        if swap is None:
            march_all(table, volume_ref, out_ref, k)
            part = (slice(None), SLABS - 1 - k)
        else:
            side = lax.axis_index("side") ^ swap
            march_rows(table, volume_ref, out_ref, side, k * piece // 16, (k + 1) * piece // 16)
            part = (slice(None), pl.ds(k * piece // 2, piece // 2))
        copies.append(pltpu.make_async_copy(out_ref.at[*part], out_any.at[*part], sems.at[2 + SLABS + k]))
        copies[-1].start()
    for copy in copies[2 + SLABS :]:
        copy.wait()


def march(colors, extinction, volume, depth_total, swap):
    _, row_count, col_count = volume.shape
    if swap is None:
        shape = (len(RANK), SLABS, 2, 8, col_count)
    else:
        shape = (4, row_count // 2, col_count)
    return pl.pallas_call(
        functools.partial(march_kernel, depth_total=depth_total, swap=swap),
        out_shape=jax.ShapeDtypeStruct(shape, jnp.float32),
        in_specs=[ANY, ANY, ANY],
        out_specs=ANY,
        scratch_shapes=[
            pltpu.VMEM(colors.shape, jnp.float32),
            pltpu.VMEM(extinction.shape, jnp.float32),
            pltpu.VMEM(volume.shape, jnp.int32),
            pltpu.VMEM(shape, jnp.float32),
            pltpu.SemaphoreType.DMA((2 + 2 * SLABS,)),
        ],
        compiler_params=pltpu.CompilerParams(vmem_limit_bytes=LARGE),
        cost_estimate=pl.CostEstimate(flops=20_000_000, bytes_accessed=8_000_000, transcendentals=0),
        name="march_all" if swap is None else "march_side%d" % swap,
    )(colors, extinction, volume)


def blend(front, back):
    clear = 1.0 - front[3]
    return [f + clear * b for f, b in zip(front, back)]


def merge_kernel(own_ref, other_ref, out_ref, *, slots):
    _, row_count, col_count = own_ref.shape
    side = lax.axis_index("side")
    odd = jnp.full((8, LANES), side) == 1
    for block in range(row_count // 8):
        places = [
            jnp.where(side == 0, slots[4 * block + even], slots[4 * block + uneven])
            for even, uneven in zip((0, 2, 1, 3), (3, 0, 2, 1))
        ]
        for col in range(0, col_count, LANES):
            at = (pl.ds(block * 8, 8), pl.ds(col, LANES))
            own = [own_ref[c, *at] for c in range(4)]
            other = [other_ref[c, *at] for c in range(4)]
            image = blend(
                [jnp.where(odd, y, x) for x, y in zip(own, other)],
                [jnp.where(odd, x, y) for x, y in zip(own, other)],
            )
            for k in range(4):
                for c in range(4):
                    out_ref[places[k], 2 * c : 2 * c + 2, pl.ds(col, LANES)] = image[c][2 * k : 2 * k + 2]


def blend_packed(front, back):
    sub = lax.broadcasted_iota(jnp.int32, front.shape, 0)
    opacity = jnp.where(sub >= 6, front, 0.0)
    opacity = opacity + pltpu.roll(opacity, 4, 0)
    opacity = opacity + pltpu.roll(opacity, 2, 0)
    return front + (1.0 - opacity) * back


def fold(parts):
    while len(parts) > 1:
        parts = [blend_packed(f, b) for f, b in zip(parts[0::2], parts[1::2])]
    return parts[0]


def fold_kernel(parts_ref, out_ref, *, slots):
    _, _, col_count = parts_ref.shape
    for col in range(0, col_count, LANES):
        image = fold([parts_ref[slot, :, pl.ds(col, LANES)] for slot in slots])
        for t in range(out_ref.shape[0]):
            out_ref[t, :, pl.ds(col, LANES)] = image


def assemble_kernel(strips_ref, out_ref):
    count, _, col_count = strips_ref.shape
    for t in range(count):
        for c in range(4):
            out_ref[c, :, pl.ds(t * col_count, col_count)] = strips_ref[count - 1 - t, 2 * c : 2 * c + 2, :]


def small_call(kernel, out_shape, name, *args):
    return pl.pallas_call(
        kernel,
        out_shape=jax.ShapeDtypeStruct(out_shape, jnp.float32),
        in_specs=[VMEM] * len(args),
        out_specs=VMEM,
        compiler_params=pltpu.CompilerParams(vmem_limit_bytes=SMALL),
        name=name,
    )(*args)


def body(volume, colors, extinction):
    tile_count = lax.axis_size("tile")
    pair_count = lax.axis_size("pair")
    depth_cells, row_count, col_count = volume.shape
    depth_total = depth_cells * 2 * pair_count
    extinction = extinction.reshape(1, -1)
    order = send_order()
    slots = [order.index(pair) for pair in range(pair_count)]

    strip_shape = (tile_count, 8, col_count)
    order64 = [2 * p + s for p in order for s in (0, 1)]

    def direct():
        image = march(colors, extinction, volume, depth_total, None).reshape(row_count // 2, 8, col_count)
        parts = lax.all_to_all(image, DEPTH, split_axis=0, concat_axis=0, tiled=True, axis_index_groups=[order64])
        f = functools.partial(fold_kernel, slots=[order64.index(d) for d in range(2 * pair_count)])
        return small_call(f, strip_shape, "fold_direct", parts)

    def paired():
        outgoing = march(colors, extinction, volume, depth_total, 1)
        other = lax.ppermute(outgoing, "side", [(0, 1), (1, 0)])
        own = march(colors, extinction, volume, depth_total, 0)
        merge = functools.partial(merge_kernel, slots=slots)
        image = small_call(merge, (row_count // 4, 8, col_count), "merge", own, other)
        parts = lax.all_to_all(image, "pair", split_axis=0, concat_axis=0, tiled=True, axis_index_groups=[order])
        fold_parts = functools.partial(fold_kernel, slots=slots)
        return small_call(fold_parts, strip_shape, "fold", parts)

    strip = lax.cond(lax.axis_index("tile") % 2 == 1, direct, paired)
    tiles = list(reversed(range(tile_count)))
    strips = lax.all_to_all(strip, "tile", split_axis=0, concat_axis=0, tiled=True, axis_index_groups=[tiles])
    return small_call(assemble_kernel, (4, 2, tile_count * col_count), "assemble", strips)


def solution(mesh):
    tiles, depth = mesh.devices.shape
    mesh = Mesh(mesh.devices.reshape(tiles, depth // SIDES, SIDES), ("tile",) + DEPTH)
    in_specs = (P(DEPTH, None, "tile"), P(), P())
    out_specs = P(None, DEPTH, None)
    return jax.shard_map(body, mesh=mesh, in_specs=in_specs, out_specs=out_specs, check_vma=False)
```

```python
import functools

import jax
import jax.numpy as jnp
from jax import lax
from jax.experimental import pallas as pl
from jax.experimental.pallas import tpu as pltpu
from jax.sharding import Mesh
from jax.sharding import PartitionSpec as P

LANES = 128
SIDES = 2
DEPTH = ("pair", "side")
SLABS = 4
UNIT = 2.0**31
RANK = (5, 7, 4, 6, 1, 3, 0, 2)
VMEM = pl.BlockSpec(memory_space=pltpu.VMEM)
ANY = pl.BlockSpec(memory_space=pl.ANY)
SMALL = 16 * 2**20
LARGE = 2**26


def send_order():
    return [x * len(RANK) + z for z in RANK for x in reversed(range(SLABS))]


def lookup(halves, bins, high):
    low_part = jnp.take_along_axis(halves[0], bins, axis=1, mode="promise_in_bounds")
    high_part = jnp.take_along_axis(halves[1], bins, axis=1, mode="promise_in_bounds")
    return jnp.where(high, high_part, low_part)


def encode(row):
    whole = jnp.round(row * UNIT).astype(jnp.int32)
    shift = sum((whole >= 256 << k).astype(jnp.int32) for k in range(22))
    return (whole >> shift) | (shift << 8)


def decode(words):
    low = (words & 255) << ((words >> 8) & 31)
    high = ((words >> 13) & 255) << (words >> 21)
    return low.astype(jnp.float32), high.astype(jnp.float32)


def table_rows(colors, extinction, depth_total):
    opacity = 1.0 - jnp.exp(-extinction / depth_total)
    rows = [colors[c : c + 1, :] * opacity for c in range(3)] + [opacity]
    codes = [encode(row.astype(jnp.bfloat16).astype(jnp.float32)) for row in rows]
    words = [codes[0] | (codes[1] << 13), codes[2] | (codes[3] << 13)]
    return [
        [jnp.broadcast_to(word[:, h * LANES : (h + 1) * LANES], (8, LANES)) for h in range(2)]
        for word in words
    ]


def by_rows(image):
    place = lax.broadcasted_iota(jnp.int32, image[0].shape, 0) // 2
    odd, upper = place % 2 == 1, place >= 2
    halves = []
    for a, b in (image[:2], image[2:]):
        halves.append((jnp.where(odd, pltpu.roll(b, 2, 0), a), jnp.where(odd, b, pltpu.roll(a, 6, 0))))
    rows = [None] * 4
    for k in range(2):
        a, b = halves[0][k], halves[1][k]
        rows[k] = jnp.where(upper, pltpu.roll(b, 4, 0), a)
        rows[k + 2] = jnp.where(upper, b, pltpu.roll(a, 4, 0))
    return rows


def march_rows(table, volume_ref, out_ref, side, lo, hi):
    depth_cells, _, col_count = volume_ref.shape
    col_blocks = col_count // LANES
    place = lax.broadcasted_iota(jnp.int32, (8, LANES), 0) // 2 % SIDES
    takes = [place == (side + j) % SIDES for j in range(1, SIDES)]

    def step(i, carry):
        block = i // col_blocks
        row = pl.multiple_of(block * 8 * SIDES, 8 * SIDES)
        col = pl.multiple_of(i % col_blocks * LANES, LANES)
        image, clear = None, None
        for z in range(depth_cells):
            bins = volume_ref[z, pl.ds(row, 8), pl.ds(col, LANES)]
            for j in range(1, SIDES):
                other = volume_ref[z, pl.ds(row + 8 * j, 8), pl.ds(col, LANES)]
                bins = jnp.where(takes[j - 1], pltpu.roll(other, 2 * j, 0), bins)
            high = bins >= LANES
            low_bits = bins & (LANES - 1)
            sample = [x for halves in table for x in decode(lookup(halves, low_bits, high))]
            if z == 0:
                image = sample
            else:
                image = [x + clear * s for x, s in zip(image, sample)]
            clear = 1.0 - image[3] * (1 / UNIT)
        for c in range(4):
            out_ref[c, pl.ds(pl.multiple_of(block * 8, 8), 8), pl.ds(col, LANES)] = image[c] * (1 / UNIT)
        return carry

    lax.fori_loop(lo * col_blocks, hi * col_blocks, step, 0, unroll=4)


def march_all(table, volume_ref, out_ref, slab):
    depth_cells, _, col_count = volume_ref.shape

    def step(i, carry):
        col = pl.multiple_of(i * LANES, LANES)
        for j in range(4):
            row = (slab * 4 + j) * 8
            image, clear = None, None
            for z in range(depth_cells):
                bins = volume_ref[z, pl.ds(row, 8), pl.ds(col, LANES)]
                high = bins >= LANES
                low_bits = bins & (LANES - 1)
                sample = [x for halves in table for x in decode(lookup(halves, low_bits, high))]
                if z == 0:
                    image = sample
                else:
                    image = [x + clear * s for x, s in zip(image, sample)]
                clear = 1.0 - image[3] * (1 / UNIT)
            for k, rows in enumerate(by_rows([x * (1 / UNIT) for x in image])):
                out_ref[k % 2, RANK.index(2 * j + k // 2), SLABS - 1 - slab, :, pl.ds(col, LANES)] = rows
        return carry

    lax.fori_loop(0, col_count // LANES, step, 0, unroll=2)


def march_kernel(
    colors_any,
    extinction_any,
    volume_any,
    out_any,
    colors_ref,
    extinction_ref,
    volume_ref,
    out_ref,
    sems,
    *,
    depth_total,
    swap,
):
    piece = volume_ref.shape[1] // SLABS
    copies = [
        pltpu.make_async_copy(colors_any, colors_ref, sems.at[0]),
        pltpu.make_async_copy(extinction_any, extinction_ref, sems.at[1]),
    ]
    for k in range(SLABS):
        rows = pl.ds(k * piece, piece)
        copies.append(
            pltpu.make_async_copy(volume_any.at[:, rows, :], volume_ref.at[:, rows, :], sems.at[2 + k])
        )
    for copy in copies:
        copy.start()
    copies[0].wait()
    copies[1].wait()
    table = table_rows(colors_ref[...], extinction_ref[...], depth_total)
    for k in range(SLABS):
        copies[2 + k].wait()
        if swap is None:
            march_all(table, volume_ref, out_ref, k)
            part = (slice(None), slice(None), SLABS - 1 - k)
        else:
            side = lax.axis_index("side") ^ swap
            march_rows(table, volume_ref, out_ref, side, k * piece // 16, (k + 1) * piece // 16)
            part = (slice(None), pl.ds(k * piece // 2, piece // 2))
        copies.append(pltpu.make_async_copy(out_ref.at[*part], out_any.at[*part], sems.at[2 + SLABS + k]))
        copies[-1].start()
    for copy in copies[2 + SLABS :]:
        copy.wait()


def march(colors, extinction, volume, depth_total, swap):
    _, row_count, col_count = volume.shape
    if swap is None:
        shape = (2, len(RANK), SLABS, 8, col_count)
    else:
        shape = (4, row_count // 2, col_count)
    return pl.pallas_call(
        functools.partial(march_kernel, depth_total=depth_total, swap=swap),
        out_shape=jax.ShapeDtypeStruct(shape, jnp.float32),
        in_specs=[ANY, ANY, ANY],
        out_specs=ANY,
        scratch_shapes=[
            pltpu.VMEM(colors.shape, jnp.float32),
            pltpu.VMEM(extinction.shape, jnp.float32),
            pltpu.VMEM(volume.shape, jnp.int32),
            pltpu.VMEM(shape, jnp.float32),
            pltpu.SemaphoreType.DMA((2 + 2 * SLABS,)),
        ],
        compiler_params=pltpu.CompilerParams(vmem_limit_bytes=LARGE),
        cost_estimate=pl.CostEstimate(flops=20_000_000, bytes_accessed=8_000_000, transcendentals=0),
        name="march_all" if swap is None else "march_side%d" % swap,
    )(colors, extinction, volume)


def blend(front, back):
    clear = 1.0 - front[3]
    return [f + clear * b for f, b in zip(front, back)]


def merge_kernel(own_ref, other_ref, out_ref, *, slots):
    _, row_count, col_count = own_ref.shape
    side = lax.axis_index("side")
    odd = jnp.full((8, LANES), side) == 1
    for block in range(row_count // 8):
        places = [
            jnp.where(side == 0, slots[4 * block + even], slots[4 * block + uneven])
            for even, uneven in zip((0, 2, 1, 3), (3, 0, 2, 1))
        ]
        for col in range(0, col_count, LANES):
            at = (pl.ds(block * 8, 8), pl.ds(col, LANES))
            own = [own_ref[c, *at] for c in range(4)]
            other = [other_ref[c, *at] for c in range(4)]
            image = blend(
                [jnp.where(odd, y, x) for x, y in zip(own, other)],
                [jnp.where(odd, x, y) for x, y in zip(own, other)],
            )
            for place, rows in zip(places, by_rows(image)):
                out_ref[place, :, pl.ds(col, LANES)] = rows


def blend_packed(front, back):
    sub = lax.broadcasted_iota(jnp.int32, front.shape, 0)
    opacity = jnp.where(sub >= 6, front, 0.0)
    opacity = opacity + pltpu.roll(opacity, 4, 0)
    opacity = opacity + pltpu.roll(opacity, 2, 0)
    return front + (1.0 - opacity) * back


def fold(parts):
    while len(parts) > 1:
        parts = [blend_packed(f, b) for f, b in zip(parts[0::2], parts[1::2])]
    return parts[0]


def fold_kernel(parts_ref, out_ref, *, slots):
    _, _, col_count = parts_ref.shape
    for col in range(0, col_count, LANES):
        image = fold([parts_ref[slot, :, pl.ds(col, LANES)] for slot in slots])
        for t in range(out_ref.shape[0]):
            out_ref[t, :, pl.ds(col, LANES)] = image


def assemble_kernel(strips_ref, out_ref):
    count, _, col_count = strips_ref.shape
    for t in range(count):
        for c in range(4):
            out_ref[c, :, pl.ds(t * col_count, col_count)] = strips_ref[count - 1 - t, 2 * c : 2 * c + 2, :]


def small_call(kernel, out_shape, name, *args):
    return pl.pallas_call(
        kernel,
        out_shape=jax.ShapeDtypeStruct(out_shape, jnp.float32),
        in_specs=[VMEM] * len(args),
        out_specs=VMEM,
        compiler_params=pltpu.CompilerParams(vmem_limit_bytes=SMALL),
        name=name,
    )(*args)


def body(volume, colors, extinction):
    tile_count = lax.axis_size("tile")
    pair_count = lax.axis_size("pair")
    depth_cells, row_count, col_count = volume.shape
    depth_total = depth_cells * 2 * pair_count
    extinction = extinction.reshape(1, -1)
    order = send_order()
    slots = [order.index(pair) for pair in range(pair_count)]

    strip_shape = (tile_count, 8, col_count)
    order64 = [2 * p + s for s in (0, 1) for p in order]

    def direct():
        image = march(colors, extinction, volume, depth_total, None).reshape(row_count // 2, 8, col_count)
        parts = lax.all_to_all(image, DEPTH, split_axis=0, concat_axis=0, tiled=True, axis_index_groups=[order64])
        f = functools.partial(fold_kernel, slots=[order64.index(d) for d in range(2 * pair_count)])
        return small_call(f, strip_shape, "fold_direct", parts)

    def paired():
        outgoing = march(colors, extinction, volume, depth_total, 1)
        other = lax.ppermute(outgoing, "side", [(0, 1), (1, 0)])
        own = march(colors, extinction, volume, depth_total, 0)
        merge = functools.partial(merge_kernel, slots=slots)
        image = small_call(merge, (row_count // 4, 8, col_count), "merge", own, other)
        parts = lax.all_to_all(image, "pair", split_axis=0, concat_axis=0, tiled=True, axis_index_groups=[order])
        fold_parts = functools.partial(fold_kernel, slots=slots)
        return small_call(fold_parts, strip_shape, "fold", parts)

    strip = lax.cond(lax.axis_index("tile") % 2 == 1, direct, paired)
    tiles = list(reversed(range(tile_count)))
    strips = lax.all_to_all(strip, "tile", split_axis=0, concat_axis=0, tiled=True, axis_index_groups=[tiles])
    return small_call(assemble_kernel, (4, 2, tile_count * col_count), "assemble", strips)


def solution(mesh):
    tiles, depth = mesh.devices.shape
    mesh = Mesh(mesh.devices.reshape(tiles, depth // SIDES, SIDES), ("tile",) + DEPTH)
    in_specs = (P(DEPTH, None, "tile"), P(), P())
    out_specs = P(None, DEPTH, None)
    return jax.shard_map(body, mesh=mesh, in_specs=in_specs, out_specs=out_specs, check_vma=False)
```

```python
import functools

import jax
import jax.numpy as jnp
from jax import lax
from jax.experimental import pallas as pl
from jax.experimental.pallas import tpu as pltpu
from jax.sharding import Mesh
from jax.sharding import PartitionSpec as P

LANES = 128
SIDES = 2
DEPTH = ("pair", "side")
SLABS = 4
UNIT = 2.0**31
RANK = (5, 7, 4, 6, 1, 3, 0, 2)
Z_RANK = (11, 15, 9, 13, 3, 7, 1, 5, 10, 14, 8, 12, 2, 6, 0, 4)
VMEM = pl.BlockSpec(memory_space=pltpu.VMEM)
ANY = pl.BlockSpec(memory_space=pl.ANY)
SMALL = 16 * 2**20
LARGE = 2**26


def send_order():
    return [x * len(RANK) + z for z in RANK for x in reversed(range(SLABS))]


def lookup(halves, bins, high):
    low_part = jnp.take_along_axis(halves[0], bins, axis=1, mode="promise_in_bounds")
    high_part = jnp.take_along_axis(halves[1], bins, axis=1, mode="promise_in_bounds")
    return jnp.where(high, high_part, low_part)


def encode(rows):
    whole = jnp.round(rows * UNIT).astype(jnp.int32)
    shift = jnp.zeros_like(whole)
    for step in (16, 8, 4, 2, 1):
        large = whole >= 1 << (7 + step)
        whole = jnp.where(large, whole >> step, whole)
        shift = jnp.where(large, shift + step, shift)
    return whole | (shift << 8)


def decode(words):
    low = (words & 255) << ((words >> 8) & 31)
    high = ((words >> 13) & 255) << (words >> 21)
    return low.astype(jnp.float32), high.astype(jnp.float32)


def table_rows(colors, extinction, depth_total, packed):
    opacity = 1.0 - jnp.exp(-extinction / depth_total)
    tints = (colors * opacity).astype(jnp.bfloat16).astype(jnp.float32)
    opacity = opacity.astype(jnp.bfloat16).astype(jnp.float32)
    if packed:
        tints, opacity = encode(tints), encode(opacity)
        words = [tints[0:1] | (tints[1:2] << 13), tints[2:3] | (opacity << 13)]
    else:
        words = [tints[0:1], tints[1:2], tints[2:3], opacity]
    return [
        [jnp.broadcast_to(word[:, h * LANES : (h + 1) * LANES], (8, LANES)) for h in range(2)]
        for word in words
    ]


def by_rows(image):
    place = lax.broadcasted_iota(jnp.int32, image[0].shape, 0) // 2
    odd, upper = place % 2 == 1, place >= 2
    halves = []
    for a, b in (image[:2], image[2:]):
        halves.append((jnp.where(odd, pltpu.roll(b, 2, 0), a), jnp.where(odd, b, pltpu.roll(a, 6, 0))))
    rows = [None] * 4
    for k in range(2):
        a, b = halves[0][k], halves[1][k]
        rows[k] = jnp.where(upper, pltpu.roll(b, 4, 0), a)
        rows[k + 2] = jnp.where(upper, b, pltpu.roll(a, 4, 0))
    return rows


def march_rows(table, volume_ref, out_ref, side, lo, hi):
    depth_cells, _, col_count = volume_ref.shape
    col_blocks = col_count // LANES
    place = lax.broadcasted_iota(jnp.int32, (8, LANES), 0) // 2 % SIDES
    takes = [place == (side + j) % SIDES for j in range(1, SIDES)]

    def step(i, carry):
        block = i // col_blocks
        row = pl.multiple_of(block * 8 * SIDES, 8 * SIDES)
        col = pl.multiple_of(i % col_blocks * LANES, LANES)
        image, clear = None, None
        for z in range(depth_cells):
            bins = volume_ref[z, pl.ds(row, 8), pl.ds(col, LANES)]
            for j in range(1, SIDES):
                other = volume_ref[z, pl.ds(row + 8 * j, 8), pl.ds(col, LANES)]
                bins = jnp.where(takes[j - 1], pltpu.roll(other, 2 * j, 0), bins)
            high = bins >= LANES
            low_bits = bins & (LANES - 1)
            sample = [x for halves in table for x in decode(lookup(halves, low_bits, high))]
            if z == 0:
                image = sample
            else:
                image = [x + clear * s for x, s in zip(image, sample)]
            clear = 1.0 - image[3] * (1 / UNIT)
        for c in range(4):
            out_ref[c, pl.ds(pl.multiple_of(block * 8, 8), 8), pl.ds(col, LANES)] = image[c] * (1 / UNIT)
        return carry

    lax.fori_loop(lo * col_blocks, hi * col_blocks, step, 0, unroll=4)


def march_all(table, volume_ref, out_ref, slab):
    depth_cells, _, col_count = volume_ref.shape

    def step(i, carry):
        col = pl.multiple_of(i * LANES, LANES)
        for j in range(4):
            row = (slab * 4 + j) * 8
            image, clear = None, None
            for z in range(depth_cells):
                bins = volume_ref[z, pl.ds(row, 8), pl.ds(col, LANES)]
                high = bins >= LANES
                low_bits = bins & (LANES - 1)
                sample = [lookup(halves, low_bits, high) for halves in table]
                if z == 0:
                    image = sample
                else:
                    image = [x + clear * s for x, s in zip(image, sample)]
                clear = 1.0 - image[3]
            for k, rows in enumerate(by_rows(image)):
                out_ref[Z_RANK.index(4 * j + k), SLABS - 1 - slab, :, pl.ds(col, LANES)] = rows
        return carry

    lax.fori_loop(0, col_count // LANES, step, 0, unroll=2)


def march_kernel(
    colors_any,
    extinction_any,
    volume_any,
    out_any,
    colors_ref,
    extinction_ref,
    volume_ref,
    out_ref,
    sems,
    *,
    depth_total,
    swap,
):
    piece = volume_ref.shape[1] // SLABS
    copies = [
        pltpu.make_async_copy(colors_any, colors_ref, sems.at[0]),
        pltpu.make_async_copy(extinction_any, extinction_ref, sems.at[1]),
    ]
    for k in range(SLABS):
        rows = pl.ds(k * piece, piece)
        copies.append(
            pltpu.make_async_copy(volume_any.at[:, rows, :], volume_ref.at[:, rows, :], sems.at[2 + k])
        )
    for copy in copies:
        copy.start()
    copies[0].wait()
    copies[1].wait()
    table = table_rows(colors_ref[...], extinction_ref[...], depth_total, swap is not None)
    for k in range(SLABS):
        copies[2 + k].wait()
        if swap is None:
            march_all(table, volume_ref, out_ref, k)
            part = (slice(None), SLABS - 1 - k)
        else:
            side = lax.axis_index("side") ^ swap
            march_rows(table, volume_ref, out_ref, side, k * piece // 16, (k + 1) * piece // 16)
            part = (slice(None), pl.ds(k * piece // 2, piece // 2))
        copies.append(pltpu.make_async_copy(out_ref.at[*part], out_any.at[*part], sems.at[2 + SLABS + k]))
        copies[-1].start()
    for copy in copies[2 + SLABS :]:
        copy.wait()


def march(colors, extinction, volume, depth_total, swap):
    _, row_count, col_count = volume.shape
    if swap is None:
        shape = (len(Z_RANK), SLABS, 8, col_count)
    else:
        shape = (4, row_count // 2, col_count)
    return pl.pallas_call(
        functools.partial(march_kernel, depth_total=depth_total, swap=swap),
        out_shape=jax.ShapeDtypeStruct(shape, jnp.float32),
        in_specs=[ANY, ANY, ANY],
        out_specs=ANY,
        scratch_shapes=[
            pltpu.VMEM(colors.shape, jnp.float32),
            pltpu.VMEM(extinction.shape, jnp.float32),
            pltpu.VMEM(volume.shape, jnp.int32),
            pltpu.VMEM(shape, jnp.float32),
            pltpu.SemaphoreType.DMA((2 + 2 * SLABS,)),
        ],
        compiler_params=pltpu.CompilerParams(vmem_limit_bytes=LARGE),
        cost_estimate=pl.CostEstimate(flops=20_000_000, bytes_accessed=8_000_000, transcendentals=0),
        name="march_all" if swap is None else "march_side%d" % swap,
    )(colors, extinction, volume)


def blend(front, back):
    clear = 1.0 - front[3]
    return [f + clear * b for f, b in zip(front, back)]


def merge_kernel(own_ref, other_ref, out_ref, *, slots):
    _, row_count, col_count = own_ref.shape
    side = lax.axis_index("side")
    odd = jnp.full((8, LANES), side) == 1
    for block in range(row_count // 8):
        places = [
            jnp.where(side == 0, slots[4 * block + even], slots[4 * block + uneven])
            for even, uneven in zip((0, 2, 1, 3), (3, 0, 2, 1))
        ]
        for col in range(0, col_count, LANES):
            at = (pl.ds(block * 8, 8), pl.ds(col, LANES))
            own = [own_ref[c, *at] for c in range(4)]
            other = [other_ref[c, *at] for c in range(4)]
            image = blend(
                [jnp.where(odd, y, x) for x, y in zip(own, other)],
                [jnp.where(odd, x, y) for x, y in zip(own, other)],
            )
            for place, rows in zip(places, by_rows(image)):
                out_ref[place, :, pl.ds(col, LANES)] = rows


def blend_packed(front, back):
    sub = lax.broadcasted_iota(jnp.int32, front.shape, 0)
    opacity = jnp.where(sub >= 6, front, 0.0)
    opacity = opacity + pltpu.roll(opacity, 4, 0)
    opacity = opacity + pltpu.roll(opacity, 2, 0)
    return front + (1.0 - opacity) * back


def fold(parts):
    while len(parts) > 1:
        parts = [blend_packed(f, b) for f, b in zip(parts[0::2], parts[1::2])]
    return parts[0]


def fold_kernel(parts_ref, out_ref, *, slots):
    _, _, col_count = parts_ref.shape
    for col in range(0, col_count, LANES):
        image = fold([parts_ref[slot, :, pl.ds(col, LANES)] for slot in slots])
        for t in range(out_ref.shape[0]):
            out_ref[t, :, pl.ds(col, LANES)] = image


def fold_slab_kernel(parts_ref, out_ref, *, slots):
    slabs, _, col_count = out_ref.shape
    for x in range(slabs):
        for col in range(0, col_count, LANES):
            parts = [parts_ref[slot * slabs + x, :, pl.ds(col, LANES)] for slot in slots]
            out_ref[x, :, pl.ds(col, LANES)] = fold(parts)


def assemble_kernel(strips_ref, out_ref):
    count, _, col_count = strips_ref.shape
    for t in range(count):
        for c in range(4):
            out_ref[c, :, pl.ds(t * col_count, col_count)] = strips_ref[count - 1 - t, 2 * c : 2 * c + 2, :]


def small_call(kernel, out_shape, name, *args):
    return pl.pallas_call(
        kernel,
        out_shape=jax.ShapeDtypeStruct(out_shape, jnp.float32),
        in_specs=[VMEM] * len(args),
        out_specs=VMEM,
        compiler_params=pltpu.CompilerParams(vmem_limit_bytes=SMALL),
        name=name,
    )(*args)


def body(volume, colors, extinction):
    tile_count = lax.axis_size("tile")
    pair_count = lax.axis_size("pair")
    depth_cells, row_count, col_count = volume.shape
    depth_total = depth_cells * 2 * pair_count
    extinction = extinction.reshape(1, -1)
    order = send_order()
    slots = [order.index(pair) for pair in range(pair_count)]

    strip_shape = (tile_count, 8, col_count)
    def direct():
        image = march(colors, extinction, volume, depth_total, None).reshape(row_count // 2, 8, col_count)
        ring = len(Z_RANK)
        along_z = [[x * ring + z for z in Z_RANK] for x in range(SLABS)]
        parts = lax.all_to_all(image, DEPTH, split_axis=0, concat_axis=0, tiled=True, axis_index_groups=along_z)
        f = functools.partial(fold_slab_kernel, slots=[Z_RANK.index(z) for z in range(ring)])
        slabs = small_call(f, (SLABS, 8, col_count), "fold_z", parts)
        along_x = [[x * ring + z for x in reversed(range(SLABS))] for z in range(ring)]
        parts = lax.all_to_all(slabs, DEPTH, split_axis=0, concat_axis=0, tiled=True, axis_index_groups=along_x)
        f = functools.partial(fold_kernel, slots=list(reversed(range(SLABS))))
        return small_call(f, strip_shape, "fold_x", parts)

    def paired():
        outgoing = march(colors, extinction, volume, depth_total, 1)
        other = lax.ppermute(outgoing, "side", [(0, 1), (1, 0)])
        own = march(colors, extinction, volume, depth_total, 0)
        merge = functools.partial(merge_kernel, slots=slots)
        image = small_call(merge, (row_count // 4, 8, col_count), "merge", own, other)
        parts = lax.all_to_all(image, "pair", split_axis=0, concat_axis=0, tiled=True, axis_index_groups=[order])
        fold_parts = functools.partial(fold_kernel, slots=slots)
        return small_call(fold_parts, strip_shape, "fold", parts)

    strip = lax.cond(lax.axis_index("tile") % 2 == 1, direct, paired)
    tiles = list(reversed(range(tile_count)))
    strips = lax.all_to_all(strip, "tile", split_axis=0, concat_axis=0, tiled=True, axis_index_groups=[tiles])
    return small_call(assemble_kernel, (4, 2, tile_count * col_count), "assemble", strips)


def solution(mesh):
    tiles, depth = mesh.devices.shape
    mesh = Mesh(mesh.devices.reshape(tiles, depth // SIDES, SIDES), ("tile",) + DEPTH)
    in_specs = (P(DEPTH, None, "tile"), P(), P())
    out_specs = P(None, DEPTH, None)
    return jax.shard_map(body, mesh=mesh, in_specs=in_specs, out_specs=out_specs, check_vma=False)
```

```python
import functools

import jax
import jax.numpy as jnp
from jax import lax
from jax.experimental import pallas as pl
from jax.experimental.pallas import tpu as pltpu
from jax.sharding import Mesh
from jax.sharding import PartitionSpec as P

LANES = 128
SIDES = 2
DEPTH = ("pair", "side")
SLABS = 4
UNIT = 2.0**31
RANK = (5, 7, 4, 6, 1, 3, 0, 2)
VMEM = pl.BlockSpec(memory_space=pltpu.VMEM)
ANY = pl.BlockSpec(memory_space=pl.ANY)
SMALL = 16 * 2**20
LARGE = 2**26


def send_order():
    return [x * len(RANK) + z for z in RANK for x in reversed(range(SLABS))]


def lookup(halves, bins, high):
    low_part = jnp.take_along_axis(halves[0], bins, axis=1, mode="promise_in_bounds")
    high_part = jnp.take_along_axis(halves[1], bins, axis=1, mode="promise_in_bounds")
    return jnp.where(high, high_part, low_part)


def encode(rows):
    whole = jnp.round(rows * UNIT).astype(jnp.int32)
    shift = jnp.zeros_like(whole)
    for step in (16, 8, 4, 2, 1):
        large = whole >= 1 << (7 + step)
        whole = jnp.where(large, whole >> step, whole)
        shift = jnp.where(large, shift + step, shift)
    return whole | (shift << 8)


def decode(words):
    low = (words & 255) << ((words >> 8) & 31)
    high = ((words >> 13) & 255) << (words >> 21)
    return low.astype(jnp.float32), high.astype(jnp.float32)


def table_rows(colors, extinction, depth_total):
    opacity = 1.0 - jnp.exp(-extinction / depth_total)
    tints = encode((colors * opacity).astype(jnp.bfloat16).astype(jnp.float32))
    last = encode(opacity.astype(jnp.bfloat16).astype(jnp.float32))
    words = [tints[0:1] | (tints[1:2] << 13), tints[2:3] | (last << 13)]
    return [
        [jnp.broadcast_to(word[:, h * LANES : (h + 1) * LANES], (8, LANES)) for h in range(2)]
        for word in words
    ]


def by_rows(image):
    place = lax.broadcasted_iota(jnp.int32, image[0].shape, 0) // 2
    odd, upper = place % 2 == 1, place >= 2
    halves = []
    for a, b in (image[:2], image[2:]):
        halves.append((jnp.where(odd, pltpu.roll(b, 2, 0), a), jnp.where(odd, b, pltpu.roll(a, 6, 0))))
    rows = [None] * 4
    for k in range(2):
        a, b = halves[0][k], halves[1][k]
        rows[k] = jnp.where(upper, pltpu.roll(b, 4, 0), a)
        rows[k + 2] = jnp.where(upper, b, pltpu.roll(a, 4, 0))
    return rows


def march_rows(table, volume_ref, out_ref, side, lo, hi):
    depth_cells, _, col_count = volume_ref.shape
    col_blocks = col_count // LANES
    place = lax.broadcasted_iota(jnp.int32, (8, LANES), 0) // 2 % SIDES
    takes = [place == (side + j) % SIDES for j in range(1, SIDES)]

    def step(i, carry):
        block = i // col_blocks
        row = pl.multiple_of(block * 8 * SIDES, 8 * SIDES)
        col = pl.multiple_of(i % col_blocks * LANES, LANES)
        image, clear = None, None
        for z in range(depth_cells):
            bins = volume_ref[z, pl.ds(row, 8), pl.ds(col, LANES)]
            for j in range(1, SIDES):
                other = volume_ref[z, pl.ds(row + 8 * j, 8), pl.ds(col, LANES)]
                bins = jnp.where(takes[j - 1], pltpu.roll(other, 2 * j, 0), bins)
            high = bins >= LANES
            low_bits = bins & (LANES - 1)
            sample = [x for halves in table for x in decode(lookup(halves, low_bits, high))]
            if z == 0:
                image = sample
            else:
                image = [x + clear * s for x, s in zip(image, sample)]
            clear = 1.0 - image[3] * (1 / UNIT)
        for c in range(4):
            out_ref[c, pl.ds(pl.multiple_of(block * 8, 8), 8), pl.ds(col, LANES)] = image[c] * (1 / UNIT)
        return carry

    lax.fori_loop(lo * col_blocks, hi * col_blocks, step, 0, unroll=4)


def march_all(table, volume_ref, out_ref, slab):
    depth_cells, _, col_count = volume_ref.shape

    def step(i, carry):
        col = pl.multiple_of(i * LANES, LANES)
        for j in range(4):
            row = (slab * 4 + j) * 8
            image, clear = None, None
            for z in range(depth_cells):
                bins = volume_ref[z, pl.ds(row, 8), pl.ds(col, LANES)]
                high = bins >= LANES
                low_bits = bins & (LANES - 1)
                sample = [x for halves in table for x in decode(lookup(halves, low_bits, high))]
                if z == 0:
                    image = sample
                else:
                    image = [x + clear * s for x, s in zip(image, sample)]
                clear = 1.0 - image[3] * (1 / UNIT)
            for k, rows in enumerate(by_rows([x * (1 / UNIT) for x in image])):
                out_ref[1 - k % 2, RANK.index(2 * j + k // 2), SLABS - 1 - slab, :, pl.ds(col, LANES)] = rows
        return carry

    lax.fori_loop(0, col_count // LANES, step, 0, unroll=2)


def march_kernel(
    colors_any,
    extinction_any,
    volume_any,
    out_any,
    colors_ref,
    extinction_ref,
    volume_ref,
    out_ref,
    sems,
    *,
    depth_total,
    swap,
):
    piece = volume_ref.shape[1] // SLABS
    copies = [
        pltpu.make_async_copy(colors_any, colors_ref, sems.at[0]),
        pltpu.make_async_copy(extinction_any, extinction_ref, sems.at[1]),
    ]
    for k in range(SLABS):
        rows = pl.ds(k * piece, piece)
        copies.append(
            pltpu.make_async_copy(volume_any.at[:, rows, :], volume_ref.at[:, rows, :], sems.at[2 + k])
        )
    for copy in copies:
        copy.start()
    copies[0].wait()
    copies[1].wait()
    table = table_rows(colors_ref[...], extinction_ref[...], depth_total)
    for k in range(SLABS):
        copies[2 + k].wait()
        if swap is None:
            march_all(table, volume_ref, out_ref, k)
            part = (slice(None), slice(None), SLABS - 1 - k)
        else:
            side = lax.axis_index("side") ^ swap
            march_rows(table, volume_ref, out_ref, side, k * piece // 16, (k + 1) * piece // 16)
            part = (slice(None), pl.ds(k * piece // 2, piece // 2))
        copies.append(pltpu.make_async_copy(out_ref.at[*part], out_any.at[*part], sems.at[2 + SLABS + k]))
        copies[-1].start()
    for copy in copies[2 + SLABS :]:
        copy.wait()


def march(colors, extinction, volume, depth_total, swap):
    _, row_count, col_count = volume.shape
    if swap is None:
        shape = (2, len(RANK), SLABS, 8, col_count)
    else:
        shape = (4, row_count // 2, col_count)
    return pl.pallas_call(
        functools.partial(march_kernel, depth_total=depth_total, swap=swap),
        out_shape=jax.ShapeDtypeStruct(shape, jnp.float32),
        in_specs=[ANY, ANY, ANY],
        out_specs=ANY,
        scratch_shapes=[
            pltpu.VMEM(colors.shape, jnp.float32),
            pltpu.VMEM(extinction.shape, jnp.float32),
            pltpu.VMEM(volume.shape, jnp.int32),
            pltpu.VMEM(shape, jnp.float32),
            pltpu.SemaphoreType.DMA((2 + 2 * SLABS,)),
        ],
        compiler_params=pltpu.CompilerParams(vmem_limit_bytes=LARGE),
        cost_estimate=pl.CostEstimate(flops=20_000_000, bytes_accessed=8_000_000, transcendentals=0),
        name="march_all" if swap is None else "march_side%d" % swap,
    )(colors, extinction, volume)


def blend(front, back):
    clear = 1.0 - front[3]
    return [f + clear * b for f, b in zip(front, back)]


def merge_kernel(own_ref, other_ref, out_ref, *, slots):
    _, row_count, col_count = own_ref.shape
    side = lax.axis_index("side")
    odd = jnp.full((8, LANES), side) == 1
    for block in range(row_count // 8):
        places = [
            jnp.where(side == 0, slots[4 * block + even], slots[4 * block + uneven])
            for even, uneven in zip((0, 2, 1, 3), (3, 0, 2, 1))
        ]
        for col in range(0, col_count, LANES):
            at = (pl.ds(block * 8, 8), pl.ds(col, LANES))
            own = [own_ref[c, *at] for c in range(4)]
            other = [other_ref[c, *at] for c in range(4)]
            image = blend(
                [jnp.where(odd, y, x) for x, y in zip(own, other)],
                [jnp.where(odd, x, y) for x, y in zip(own, other)],
            )
            for place, rows in zip(places, by_rows(image)):
                out_ref[place, :, pl.ds(col, LANES)] = rows


def blend_packed(front, back):
    sub = lax.broadcasted_iota(jnp.int32, front.shape, 0)
    opacity = jnp.where(sub >= 6, front, 0.0)
    opacity = opacity + pltpu.roll(opacity, 4, 0)
    opacity = opacity + pltpu.roll(opacity, 2, 0)
    return front + (1.0 - opacity) * back


def fold(parts):
    while len(parts) > 1:
        parts = [blend_packed(f, b) for f, b in zip(parts[0::2], parts[1::2])]
    return parts[0]


def fold_kernel(parts_ref, out_ref, *, slots):
    _, _, col_count = parts_ref.shape
    for col in range(0, col_count, LANES):
        image = fold([parts_ref[slot, :, pl.ds(col, LANES)] for slot in slots])
        for t in range(out_ref.shape[0]):
            out_ref[t, :, pl.ds(col, LANES)] = image


def assemble_kernel(strips_ref, out_ref):
    count, _, col_count = strips_ref.shape
    for t in range(count):
        for c in range(4):
            out_ref[c, :, pl.ds(t * col_count, col_count)] = strips_ref[count - 1 - t, 2 * c : 2 * c + 2, :]


def small_call(kernel, out_shape, name, *args):
    return pl.pallas_call(
        kernel,
        out_shape=jax.ShapeDtypeStruct(out_shape, jnp.float32),
        in_specs=[VMEM] * len(args),
        out_specs=VMEM,
        compiler_params=pltpu.CompilerParams(vmem_limit_bytes=SMALL),
        name=name,
    )(*args)


def body(volume, colors, extinction):
    tile_count = lax.axis_size("tile")
    pair_count = lax.axis_size("pair")
    depth_cells, row_count, col_count = volume.shape
    depth_total = depth_cells * 2 * pair_count
    extinction = extinction.reshape(1, -1)
    order = send_order()
    slots = [order.index(pair) for pair in range(pair_count)]

    strip_shape = (tile_count, 8, col_count)
    order64 = [2 * p + s for s in (1, 0) for p in order]

    def direct():
        image = march(colors, extinction, volume, depth_total, None).reshape(row_count // 2, 8, col_count)
        parts = lax.all_to_all(image, DEPTH, split_axis=0, concat_axis=0, tiled=True, axis_index_groups=[order64])
        f = functools.partial(fold_kernel, slots=[order64.index(d) for d in range(2 * pair_count)])
        return small_call(f, strip_shape, "fold_direct", parts)

    def paired():
        outgoing = march(colors, extinction, volume, depth_total, 1)
        other = lax.ppermute(outgoing, "side", [(0, 1), (1, 0)])
        own = march(colors, extinction, volume, depth_total, 0)
        merge = functools.partial(merge_kernel, slots=slots)
        image = small_call(merge, (row_count // 4, 8, col_count), "merge", own, other)
        parts = lax.all_to_all(image, "pair", split_axis=0, concat_axis=0, tiled=True, axis_index_groups=[order])
        fold_parts = functools.partial(fold_kernel, slots=slots)
        return small_call(fold_parts, strip_shape, "fold", parts)

    strip = lax.cond(lax.axis_index("tile") % 2 == 1, direct, paired)
    tiles = list(reversed(range(tile_count)))
    strips = lax.all_to_all(strip, "tile", split_axis=0, concat_axis=0, tiled=True, axis_index_groups=[tiles])
    return small_call(assemble_kernel, (4, 2, tile_count * col_count), "assemble", strips)


def solution(mesh):
    tiles, depth = mesh.devices.shape
    mesh = Mesh(mesh.devices.reshape(tiles, depth // SIDES, SIDES), ("tile",) + DEPTH)
    in_specs = (P(DEPTH, None, "tile"), P(), P())
    out_specs = P(None, DEPTH, None)
    return jax.shard_map(body, mesh=mesh, in_specs=in_specs, out_specs=out_specs, check_vma=False)
```

```python
import functools

import jax
import jax.numpy as jnp
from jax import lax
from jax.experimental import pallas as pl
from jax.experimental.pallas import tpu as pltpu
from jax.sharding import Mesh
from jax.sharding import PartitionSpec as P

LANES = 128
SIDES = 2
DEPTH = ("pair", "side")
SLABS = 4
UNIT = 2.0**31
RANK = (5, 7, 4, 6, 1, 3, 0, 2)
VMEM = pl.BlockSpec(memory_space=pltpu.VMEM)
ANY = pl.BlockSpec(memory_space=pl.ANY)
SMALL = 16 * 2**20
LARGE = 2**26
COST = pl.CostEstimate(flops=20_000_000, bytes_accessed=8_000_000, transcendentals=0)


def send_order():
    return [x * len(RANK) + z for z in RANK for x in reversed(range(SLABS))]


def lookup(halves, bins, high):
    low_part = jnp.take_along_axis(halves[0], bins, axis=1, mode="promise_in_bounds")
    high_part = jnp.take_along_axis(halves[1], bins, axis=1, mode="promise_in_bounds")
    return jnp.where(high, high_part, low_part)


def encode(row):
    whole = jnp.round(row * UNIT).astype(jnp.int32)
    shift = sum((whole >= 256 << k).astype(jnp.int32) for k in range(22))
    return (whole >> shift) | (shift << 8)


def decode(words):
    low = (words & 255) << ((words >> 8) & 31)
    high = ((words >> 13) & 255) << (words >> 21)
    return low.astype(jnp.float32), high.astype(jnp.float32)


def table_rows(colors, extinction, depth_total):
    opacity = 1.0 - jnp.exp(-extinction / depth_total)
    rows = [colors[c : c + 1, :] * opacity for c in range(3)] + [opacity]
    codes = [encode(row.astype(jnp.bfloat16).astype(jnp.float32)) for row in rows]
    words = [codes[0] | (codes[1] << 13), codes[2] | (codes[3] << 13)]
    return [
        [jnp.broadcast_to(word[:, h * LANES : (h + 1) * LANES], (8, LANES)) for h in range(2)]
        for word in words
    ]


def by_rows(image):
    place = lax.broadcasted_iota(jnp.int32, image[0].shape, 0) // 2
    odd, upper = place % 2 == 1, place >= 2
    halves = []
    for a, b in (image[:2], image[2:]):
        halves.append((jnp.where(odd, pltpu.roll(b, 2, 0), a), jnp.where(odd, b, pltpu.roll(a, 6, 0))))
    rows = [None] * 4
    for k in range(2):
        a, b = halves[0][k], halves[1][k]
        rows[k] = jnp.where(upper, pltpu.roll(b, 4, 0), a)
        rows[k + 2] = jnp.where(upper, b, pltpu.roll(a, 4, 0))
    return rows


def march_rows(table, volume_ref, out_ref, side, lo, hi):
    depth_cells, _, col_count = volume_ref.shape
    col_blocks = col_count // LANES
    place = lax.broadcasted_iota(jnp.int32, (8, LANES), 0) // 2 % SIDES
    takes = [place == (side + j) % SIDES for j in range(1, SIDES)]

    def step(i, carry):
        block = i // col_blocks
        row = pl.multiple_of(block * 8 * SIDES, 8 * SIDES)
        col = pl.multiple_of(i % col_blocks * LANES, LANES)
        image, clear = None, None
        for z in range(depth_cells):
            bins = volume_ref[z, pl.ds(row, 8), pl.ds(col, LANES)]
            for j in range(1, SIDES):
                other = volume_ref[z, pl.ds(row + 8 * j, 8), pl.ds(col, LANES)]
                bins = jnp.where(takes[j - 1], pltpu.roll(other, 2 * j, 0), bins)
            high = bins >= LANES
            low_bits = bins & (LANES - 1)
            sample = [x for halves in table for x in decode(lookup(halves, low_bits, high))]
            if z == 0:
                image = sample
            else:
                image = [x + clear * s for x, s in zip(image, sample)]
            clear = 1.0 - image[3] * (1 / UNIT)
        for c in range(4):
            out_ref[c, pl.ds(pl.multiple_of(block * 8, 8), 8), pl.ds(col, LANES)] = image[c] * (1 / UNIT)
        return carry

    lax.fori_loop(lo * col_blocks, hi * col_blocks, step, 0, unroll=4)


def march_all(table, volume_ref, out_ref, slab):
    depth_cells, _, col_count = volume_ref.shape

    def step(i, carry):
        col = pl.multiple_of(i * LANES, LANES)
        for j in range(4):
            row = (slab * 4 + j) * 8
            image, clear = None, None
            for z in range(depth_cells):
                bins = volume_ref[z, pl.ds(row, 8), pl.ds(col, LANES)]
                high = bins >= LANES
                low_bits = bins & (LANES - 1)
                sample = [x for halves in table for x in decode(lookup(halves, low_bits, high))]
                if z == 0:
                    image = sample
                else:
                    image = [x + clear * s for x, s in zip(image, sample)]
                clear = 1.0 - image[3] * (1 / UNIT)
            for k, rows in enumerate(by_rows([x * (1 / UNIT) for x in image])):
                out_ref[k % 2, RANK.index(2 * j + k // 2), SLABS - 1 - slab, :, pl.ds(col, LANES)] = rows
        return carry

    lax.fori_loop(0, col_count // LANES, step, 0, unroll=2)


def march_kernel(
    colors_any,
    extinction_any,
    volume_any,
    out_any,
    colors_ref,
    extinction_ref,
    volume_ref,
    out_ref,
    sems,
    *,
    depth_total,
    swap,
):
    piece = volume_ref.shape[1] // SLABS
    copies = [
        pltpu.make_async_copy(colors_any, colors_ref, sems.at[0]),
        pltpu.make_async_copy(extinction_any, extinction_ref, sems.at[1]),
    ]
    for k in range(SLABS):
        rows = pl.ds(k * piece, piece)
        copies.append(
            pltpu.make_async_copy(volume_any.at[:, rows, :], volume_ref.at[:, rows, :], sems.at[2 + k])
        )
    for copy in copies:
        copy.start()
    copies[0].wait()
    copies[1].wait()
    table = table_rows(colors_ref[...], extinction_ref[...], depth_total)
    for k in range(SLABS):
        copies[2 + k].wait()
        if swap is None:
            march_all(table, volume_ref, out_ref, k)
            part = (slice(None), slice(None), SLABS - 1 - k)
        else:
            side = lax.axis_index("side") ^ swap
            march_rows(table, volume_ref, out_ref, side, k * piece // 16, (k + 1) * piece // 16)
            part = (slice(None), pl.ds(k * piece // 2, piece // 2))
        copies.append(pltpu.make_async_copy(out_ref.at[*part], out_any.at[*part], sems.at[2 + SLABS + k]))
        copies[-1].start()
    for copy in copies[2 + SLABS :]:
        copy.wait()


def march(colors, extinction, volume, depth_total, swap):
    _, row_count, col_count = volume.shape
    if swap is None:
        shape = (2, len(RANK), SLABS, 8, col_count)
    else:
        shape = (4, row_count // 2, col_count)
    return pl.pallas_call(
        functools.partial(march_kernel, depth_total=depth_total, swap=swap),
        out_shape=jax.ShapeDtypeStruct(shape, jnp.float32),
        in_specs=[ANY, ANY, ANY],
        out_specs=ANY,
        scratch_shapes=[
            pltpu.VMEM(colors.shape, jnp.float32),
            pltpu.VMEM(extinction.shape, jnp.float32),
            pltpu.VMEM(volume.shape, jnp.int32),
            pltpu.VMEM(shape, jnp.float32),
            pltpu.SemaphoreType.DMA((2 + 2 * SLABS,)),
        ],
        compiler_params=pltpu.CompilerParams(vmem_limit_bytes=LARGE),
        cost_estimate=COST,
        name="march_all" if swap is None else "march_side%d" % swap,
    )(colors, extinction, volume)


def own_kernel(colors_ref, extinction_ref, volume_ref, out_ref, *, depth_total):
    table = table_rows(colors_ref[...], extinction_ref[...], depth_total)
    march_rows(table, volume_ref, out_ref, lax.axis_index("side"), 0, volume_ref.shape[1] // 16)


def blend(front, back):
    clear = 1.0 - front[3]
    return [f + clear * b for f, b in zip(front, back)]


def merge_kernel(own_ref, other_ref, out_ref, *, slots):
    _, row_count, col_count = own_ref.shape
    side = lax.axis_index("side")
    odd = jnp.full((8, LANES), side) == 1
    for block in range(row_count // 8):
        places = [
            jnp.where(side == 0, slots[4 * block + even], slots[4 * block + uneven])
            for even, uneven in zip((0, 2, 1, 3), (3, 0, 2, 1))
        ]
        for col in range(0, col_count, LANES):
            at = (pl.ds(block * 8, 8), pl.ds(col, LANES))
            own = [own_ref[c, *at] for c in range(4)]
            other = [other_ref[c, *at] for c in range(4)]
            image = blend(
                [jnp.where(odd, y, x) for x, y in zip(own, other)],
                [jnp.where(odd, x, y) for x, y in zip(own, other)],
            )
            for place, rows in zip(places, by_rows(image)):
                out_ref[place, :, pl.ds(col, LANES)] = rows


def blend_packed(front, back):
    sub = lax.broadcasted_iota(jnp.int32, front.shape, 0)
    opacity = jnp.where(sub >= 6, front, 0.0)
    opacity = opacity + pltpu.roll(opacity, 4, 0)
    opacity = opacity + pltpu.roll(opacity, 2, 0)
    return front + (1.0 - opacity) * back


def fold(parts):
    while len(parts) > 1:
        parts = [blend_packed(f, b) for f, b in zip(parts[0::2], parts[1::2])]
    return parts[0]


def fold_kernel(parts_ref, out_ref, *, slots):
    _, _, col_count = parts_ref.shape
    for col in range(0, col_count, LANES):
        image = fold([parts_ref[slot, :, pl.ds(col, LANES)] for slot in slots])
        for t in range(out_ref.shape[0]):
            out_ref[t, :, pl.ds(col, LANES)] = image


def assemble_kernel(strips_ref, out_ref):
    count, _, col_count = strips_ref.shape
    for t in range(count):
        for c in range(4):
            out_ref[c, :, pl.ds(t * col_count, col_count)] = strips_ref[count - 1 - t, 2 * c : 2 * c + 2, :]


def small_call(kernel, out_shape, name, *args):
    return pl.pallas_call(
        kernel,
        out_shape=jax.ShapeDtypeStruct(out_shape, jnp.float32),
        in_specs=[VMEM] * len(args),
        out_specs=VMEM,
        compiler_params=pltpu.CompilerParams(vmem_limit_bytes=SMALL),
        cost_estimate=COST if name == "march_own" else None,
        name=name,
    )(*args)


def body(volume, colors, extinction):
    tile_count = lax.axis_size("tile")
    pair_count = lax.axis_size("pair")
    depth_cells, row_count, col_count = volume.shape
    depth_total = depth_cells * 2 * pair_count
    extinction = extinction.reshape(1, -1)
    order = send_order()
    slots = [order.index(pair) for pair in range(pair_count)]

    strip_shape = (tile_count, 8, col_count)
    order64 = [2 * p + s for s in (0, 1) for p in order]

    def direct():
        image = march(colors, extinction, volume, depth_total, None).reshape(row_count // 2, 8, col_count)
        parts = lax.all_to_all(image, DEPTH, split_axis=0, concat_axis=0, tiled=True, axis_index_groups=[order64])
        f = functools.partial(fold_kernel, slots=[order64.index(d) for d in range(2 * pair_count)])
        return small_call(f, strip_shape, "fold_direct", parts)

    def paired():
        outgoing = march(colors, extinction, volume, depth_total, 1)
        other = lax.ppermute(outgoing, "side", [(0, 1), (1, 0)])
        march_own = functools.partial(own_kernel, depth_total=depth_total)
        own = small_call(march_own, (4, row_count // 2, col_count), "march_own", colors, extinction, volume)
        merge = functools.partial(merge_kernel, slots=slots)
        image = small_call(merge, (row_count // 4, 8, col_count), "merge", own, other)
        parts = lax.all_to_all(image, "pair", split_axis=0, concat_axis=0, tiled=True, axis_index_groups=[order])
        fold_parts = functools.partial(fold_kernel, slots=slots)
        return small_call(fold_parts, strip_shape, "fold", parts)

    strip = lax.cond(lax.axis_index("tile") % 2 == 1, direct, paired)
    tiles = list(reversed(range(tile_count)))
    strips = lax.all_to_all(strip, "tile", split_axis=0, concat_axis=0, tiled=True, axis_index_groups=[tiles])
    return small_call(assemble_kernel, (4, 2, tile_count * col_count), "assemble", strips)


def solution(mesh):
    tiles, depth = mesh.devices.shape
    mesh = Mesh(mesh.devices.reshape(tiles, depth // SIDES, SIDES), ("tile",) + DEPTH)
    in_specs = (P(DEPTH, None, "tile"), P(), P())
    out_specs = P(None, DEPTH, None)
    return jax.shard_map(body, mesh=mesh, in_specs=in_specs, out_specs=out_specs, check_vma=False)
```
